32 devices in a mesh: gz: 4 (over y, core), xy: 8 (over z, x).
Axes of the slice: x: 2, y: 2, z: 4, core: 2. Of those that a mesh axis runs over, the one named last changes fastest.
Arguments:
- hodge: float32 [4, 4, 32, 8192], P(None, None, 'gz', 'xy')
- permeability: float32 [32, 8192], P('gz', 'xy')
- storage: float32 [32, 8192], P('gz', 'xy'), may hold values from 0.5 to 2
- pore_volume: float32 [32, 8192], P('gz', 'xy'), may hold values from 0.5 to 2
- source: float32 [32, 8192], P('gz', 'xy'), may hold values from -60 to 60
- saturation_old: float32 [32, 8192], P('gz', 'xy'), may hold values from 0 to 1
- neighbours: int32 [4, 32, 8192], P(None, 'gz', 'xy'), may hold values from 0 to 168, as said below
- upwind: int32 [8, 4, 32, 8192], P(None, None, 'gz', 'xy'), may hold values 0 or 1
- active: int32 [32, 8192], P('gz', 'xy'), may hold values 0 or 1
Outputs:
- pressure: float32 [32, 8192], P('gz', 'xy')
- saturation: float32 [32, 8192], P('gz', 'xy')
The draws below stay inside these ranges and needn't reach their ends.
Inputs may be any that keep to these rules, and one draw needn't show every extreme that they name: `neighbours`: every code names an offset that stays within the extended block of the cell and outside its corner regions; it is never the cell itself.
All inputs are finite; a program needn't handle non-finite values. No bound on the sum of `upwind` or of `active` on one device may be relied on, other than what follows from the above.
Results may differ from the reference program's by a relative error of at most 0.0001.
Values sent between devices are 32-bit elements; how exact they have to be, the bound alone decides.
A program may use at most 64 MiB of HBM per device.

```python
import jax
import jax.numpy as jnp

ROWS = 8
COLS = 1024
REACH = 6
ITERS = 4
NSUB = 8
NR = 32
NC = 8192


def draw_neighbours(key, part):
    key_row, key_col = jax.random.split(jax.random.fold_in(key, 11))
    shift_row = jax.random.randint(key_row, (4, NR, NC), -REACH, REACH + 1)
    shift_col = jax.random.randint(key_col, (4, NR, NC), -REACH, REACH + 1)
    same = (shift_row == 0) & (shift_col == 0)
    shift_col = jnp.where(same, 1, shift_col)
    rows = (jnp.arange(NR, dtype=jnp.int32) % ROWS)[None, :, None]
    cols = (jnp.arange(NC, dtype=jnp.int32) % COLS)[None, None, :]
    local_row = rows + REACH + shift_row
    local_col = cols + REACH + shift_col
    out_row = (local_row < REACH) | (local_row >= ROWS + REACH)
    out_col = (local_col < REACH) | (local_col >= COLS + REACH)
    local_col = jnp.where(out_row & out_col, cols + REACH + 0 * local_col, local_col)
    return ((local_row - rows) * (2 * REACH + 1) + (local_col - cols)).astype(jnp.int32)


def draw_hodge(key, part):
    key_diag, key_off = jax.random.split(jax.random.fold_in(key, 12))
    diag = jnp.exp(jax.random.uniform(key_diag, (4, NR, NC), jnp.float32, 0.0, 1.3862944))
    raw = jax.random.uniform(key_off, (4, 4, NR, NC), jnp.float32, -0.3, 0.3)
    off = 0.5 * (raw + jnp.swapaxes(raw, 0, 1))
    eye = (jnp.arange(4)[:, None] == jnp.arange(4)[None, :])[:, :, None, None]
    return jnp.where(eye, diag[:, None] * jnp.ones((1, 4, 1, 1), jnp.float32), off).astype(jnp.float32)


def draw_permeability(key, part):
    key_perm = jax.random.fold_in(key, 13)
    rows = jnp.arange(NR, dtype=jnp.float32)[:, None] / NR
    cols = jnp.arange(NC, dtype=jnp.float32)[None, :] / NC
    ramp = (1.0 + 2.0 * rows) * (1.0 + 2.0 * cols) / 3.0
    base = jnp.exp(jax.random.uniform(key_perm, (NR, NC), jnp.float32, -1.2039728, 1.0986123))
    return (base * ramp).astype(jnp.float32)


def touch_ends(array, key, smallest, high):
    index_at = [jax.random.randint(jax.random.fold_in(key, axis), (), 0, length) for axis, length in enumerate(array.shape)]
    main_axis = array.shape.index(max(array.shape))
    neighbour = index_at[:main_axis] + [(index_at[main_axis] + 1) % array.shape[main_axis]] + index_at[main_axis + 1:]
    return array.at[tuple(index_at)].set(smallest).at[tuple(neighbour)].set(high)


def block_scale(rng, dims, cuts, low, top_value):
    def one(position, shards_of):
        steps = jax.random.uniform(jax.random.fold_in(jax.random.fold_in(rng, 6), position), (shards_of,), jnp.float32, low / len(cuts), top_value / len(cuts))
        return jnp.repeat(jnp.exp(steps), dims[position] // shards_of).reshape((-1,) + (1,) * (len(dims) - position - 1))

    loudness = one(*cuts[0])
    for cut in cuts[1:]:
        loudness = loudness * one(*cut)
    return loudness


def bell_draw(own_key, dims, scale, bound, pieces=(), held_as=jnp.bfloat16):
    gain = block_scale(own_key, dims, pieces, -0.22, 0.18) if pieces else 1.0
    result = jax.random.normal(own_key, dims, jnp.float32) * scale * gain
    return jnp.minimum(jnp.maximum(result, -bound), bound).astype(held_as)


def setup_inputs(seed: int = 0) -> dict:
    seeds = jax.random.split(jax.random.key(seed), 10)
    hodge = draw_hodge(jax.random.fold_in(seeds[9], 71), 0)
    permeability = draw_permeability(jax.random.fold_in(seeds[9], 71), 0)
    storage = jnp.clip(0.5 + 1.5 * jax.random.uniform(seeds[2], (NR, NC), jnp.float32) ** block_scale(seeds[2], (NR, NC), ((0, 4), (1, 8)), -0.2, 0.2), 0.5, 2.0)
    pore_volume = jnp.clip(0.5 + 1.5 * jax.random.uniform(seeds[3], (NR, NC), jnp.float32) ** block_scale(seeds[3], (NR, NC), ((0, 4), (1, 8)), -0.2, 0.2), 0.5, 2.0)
    source = bell_draw(seeds[4], (NR, NC), 10.0, 60.0, ((0, 4), (1, 8)), jnp.float32)
    saturation_old = jnp.clip(1.0 * jax.random.uniform(seeds[5], (NR, NC), jnp.float32) ** block_scale(seeds[5], (NR, NC), ((0, 4), (1, 8)), -0.2, 0.2), 0.0, 1.0)
    neighbours = draw_neighbours(jax.random.fold_in(seeds[9], 71), 0)
    upwind = touch_ends((jax.random.randint(seeds[7], (NSUB, 4, NR, NC), 0, 2) < 1).astype(jnp.int32), jax.random.fold_in(seeds[7], 1), 0, 1)
    active = touch_ends((jax.random.randint(seeds[8], (NR, NC), 0, 4) < 3).astype(jnp.int32), jax.random.fold_in(seeds[8], 1), 0, 1)
    return {"hodge": hodge, "permeability": permeability, "storage": storage, "pore_volume": pore_volume, "source": source, "saturation_old": saturation_old, "neighbours": neighbours, "upwind": upwind, "active": active}


def look(field, neighbours):
    padded = jnp.pad(field, REACH)
    span = 2 * REACH + 1
    rows = jnp.arange(NR, dtype=jnp.int32)[:, None]
    cols = jnp.arange(NC, dtype=jnp.int32)[None, :]
    return padded[rows + neighbours // span, cols + neighbours % span]


def fraction(sat):
    return sat * sat / (sat * sat + 0.5 * (1.0 - sat) * (1.0 - sat))


def reference(hodge, permeability, storage, pore_volume, source, saturation_old, neighbours, upwind, active):
    coupling = permeability[None] * jnp.sum(hodge, axis=0)
    diag = storage + jnp.sum(coupling, axis=0)

    def apply_op(field):
        near = look(field, neighbours)
        return storage * field + jnp.sum(coupling * (field[None] - near), axis=0)

    theta = 1.0
    delta = 0.9
    sigma = theta / delta
    solution = jnp.zeros_like(source)
    resid = source
    direction = resid / diag / theta
    rho = 1.0 / sigma
    for step in range(ITERS):
        image = apply_op(direction)
        solution = solution + direction
        resid = resid - image
        if step < ITERS - 1:
            scaled = resid / diag
            rho_new = 1.0 / (2.0 * sigma - rho)
            direction = rho_new * rho * direction + (2.0 * rho_new / delta) * scaled
            rho = rho_new
    near = look(solution, neighbours)
    flux = permeability[None] * jnp.sum(hodge * (solution[None] - near)[None], axis=1)
    speed = jnp.abs(flux)
    rate = jnp.sum(speed, axis=0) / pore_volume
    tau = 0.8 / jnp.max(rate)
    sat = saturation_old
    live = active.astype(jnp.float32)
    for sub in range(NSUB):
        side = upwind[sub].astype(jnp.float32)
        inflow = jnp.sum(speed * (side * fraction(look(sat, neighbours)) - (1.0 - side) * fraction(sat)[None]), axis=0)
        sat = sat + live * tau * inflow / pore_volume
    return solution, sat
```

```python
import functools

import jax
import jax.numpy as jnp
from jax import lax
from jax.experimental import pallas as pl
from jax.experimental.pallas import tpu as pltpu
from jax.sharding import PartitionSpec as P

REACH = 6
SPAN = 2 * REACH + 1
ITERS = 4
NSUB = 8
FACES = 4
LANES = 128
EDGE = 2 * REACH
NEVER = 99
MESH = pl.DeviceIdType.MESH
UNROLL = 2


def fraction(sat):
    return sat * sat / (sat * sat + 0.5 * (1.0 - sat) * (1.0 - sat))


def chebyshev():
    sigma = 1.0 / 0.9
    rho = 1.0 / sigma
    pairs = []
    for _ in range(ITERS - 1):
        rho_new = 1.0 / (2.0 * sigma - rho)
        pairs.append((rho_new * rho, 2.0 * rho_new / 0.9))
        rho = rho_new
    return pairs


def take(tile, index):
    return jnp.take_along_axis(tile, index, axis=1, mode="promise_in_bounds")


def kernel(
    nz, nx, tiles,
    hodge_h, perm_h, stor_h, pv_h, src_h, sat_h, near_h, up_h, act_h,
    p_out, s_out,
    hodge, perm, stor, pv, src, sat, code, up, act,
    ext, sides, seam, rcode, gindex, coef, zed, total, nears, speed, grow, gain,
    peak, peaks_z, peaks_x,
    load_sem, send_sem, recv_sem, pz_send, pz_recv, px_send, px_recv,
):
    gz = lax.axis_index("gz")
    xy = lax.axis_index("xy")
    loads = [
        pltpu.make_async_copy(a, b, load_sem.at[i])
        for i, (a, b) in enumerate(
            [(sat_h, sat), (near_h, code), (hodge_h, hodge), (perm_h, perm), (stor_h, stor),
             (src_h, src), (pv_h, pv), (act_h, act), (up_h, up)]
        )
    ]
    for load in loads:
        load.start()

    barrier = pltpu.get_barrier_semaphore()
    for k in range(1, nz):
        pl.semaphore_signal(barrier, inc=1, device_id=(lax.rem(gz + k, nz), xy), device_id_type=MESH)
    for k in range(1, nx):
        pl.semaphore_signal(barrier, inc=1, device_id=(gz, lax.rem(xy + k, nx)), device_id_type=MESH)

    lane = lax.broadcasted_iota(jnp.int32, (8, LANES), 1)
    row = lax.broadcasted_iota(jnp.int32, (8, LANES), 0)

    def cols(t):
        return pl.ds(pl.multiple_of(t * LANES, LANES), LANES)

    def to_seam(t, tile, into):
        u = lane - (EDGE * t + REACH)
        index = jnp.where(u < REACH, u, u + (LANES - EDGE)) & (LANES - 1)
        return jnp.where((u >= 0) & (u < EDGE), take(tile, index), into)

    def from_seam(t):
        inner = jnp.where(lane >= LANES - REACH, lane + (EDGE * t + EDGE + REACH - LANES), LANES - 1)
        return jnp.where(lane < REACH, lane + (EDGE * t + REACH), inner)

    def copy(slot, side):
        source, target, device = (
            (ext.at[slot, :, 8:16, :], ext.at[slot, :, 16:24, :], (gz - 1, xy)),
            (ext.at[slot, :, 8:16, :], ext.at[slot, :, 0:8, :], (gz + 1, xy)),
            (ext.at[slot, tiles, 8:16, :], sides.at[slot, 1], (gz, xy - 1)),
            (ext.at[slot, tiles, 8:16, :], sides.at[slot, 0], (gz, xy + 1)),
        )[side]
        return pltpu.make_async_remote_copy(
            src_ref=source, dst_ref=target,
            send_sem=send_sem.at[slot, side], recv_sem=recv_sem.at[slot, side],
            device_id=device, device_id_type=MESH,
        )

    has = (gz > 0, gz < nz - 1, xy > 0, xy < nx - 1)

    def start(slot):
        for side in (2, 3, 0, 1):
            @pl.when(has[side])
            def _():
                copy(slot, side).start()

    def wait_send(slot):
        for side in range(4):
            @pl.when(has[side])
            def _():
                copy(slot, side).wait_send()

    def wait_recv(slot):
        for side in range(4):
            @pl.when(has[side ^ 1])
            def _():
                copy(slot, side).wait_recv()

    loads[0].wait()

    def first_sat(t, seams):
        value = fraction(sat[:, cols(t)])
        ext[ITERS, t, 8:16, :] = value
        return to_seam(t, value, seams)

    zero = jnp.zeros((8, LANES), jnp.float32)
    ext[ITERS, tiles, 8:16, :] = lax.fori_loop(0, tiles, first_sat, zero, unroll=UNROLL)
    pl.semaphore_wait(barrier, nz + nx - 2)
    start(ITERS)

    for load in loads[1:6]:
        load.wait()

    def setup(t, seams):
        weights = []
        for g in range(FACES):
            summed = hodge[0, g, :, cols(t)]
            for f in range(1, FACES):
                summed = summed + hodge[f, g, :, cols(t)]
            weights.append(perm[:, cols(t)] * summed)
        diag = stor[:, cols(t)] + (weights[0] + weights[1] + weights[2] + weights[3])
        for g in range(FACES):
            coef[g, t] = weights[g] / diag
        first = src[:, cols(t)] / diag
        zed[t] = first
        total[t] = first
        ext[0, t, 8:16, :] = first
        return to_seam(t, first, seams)

    ext[0, tiles, 8:16, :] = lax.fori_loop(0, tiles, setup, zero, unroll=UNROLL)
    start(0)

    def rows_code(value):
        return (value * 79) >> 10

    def outside(rc):
        at = row + rc - REACH
        return ((gz == 0) & (at < 0)) | ((gz == nz - 1) & (at >= 8))

    def codes(t, seams):
        grown = []
        for f in range(FACES):
            value = code[f, :, cols(t)]
            rc = rows_code(value)
            col = lane + (value - SPAN * rc - REACH)
            cross = (col < 0) | (col >= LANES)
            gindex[f, t] = col & (LANES - 1)
            rcode[f, t] = jnp.where(cross | outside(rc), NEVER, rc)
            grown.append(to_seam(t, value, seams[f]))
        return tuple(grown)

    seam_codes = lax.fori_loop(0, tiles, codes, (jnp.zeros((8, LANES), jnp.int32),) * FACES)
    for f in range(FACES):
        value = seam_codes[f]
        rc = rows_code(value)
        shift = value - SPAN * rc - REACH
        base = EDGE * ((lane * 43) >> 9)
        here = lane - base
        there = here + shift
        cross = jnp.where(here < REACH, there - REACH, REACH - 1 - there) >= 0
        ours = (lane >= REACH) & (lane < EDGE * tiles + REACH)
        inside = jnp.logical_not(
            ((xy == 0) & (base == 0) & (there < REACH))
            | ((xy == nx - 1) & (base == EDGE * tiles) & (there >= REACH))
        )
        gindex[f, tiles] = (lane + shift) & (LANES - 1)
        rcode[f, tiles] = jnp.where(cross & ours & inside & jnp.logical_not(outside(rc)), rc, NEVER)

    def look(load, t, begin):
        out = list(begin)
        index = [gindex[f, t] for f in range(FACES)]
        rows = [rcode[f, t] for f in range(FACES)]
        for s in range(SPAN):
            x = load(s)
            for f in range(FACES):
                out[f] = jnp.where(rows[f] == s, take(x, index[f]), out[f])
        return out

    def seam_look(slot):
        seam[0:8, :] = ext[slot, tiles, 0:8, :]
        seam[16:24, :] = ext[slot, tiles, 16:24, :]
        left = take(sides[slot, 0], (lane + EDGE * tiles) & (LANES - 1))
        right = take(sides[slot, 1], (lane - EDGE * tiles) & (LANES - 1))
        own = ext[slot, tiles, 8:16, :]
        own = jnp.where(lane < REACH, left, own)
        own = jnp.where(lane >= EDGE * tiles + REACH, right, own)
        seam[8:16, :] = own
        return look(lambda s: seam[2 + s : 10 + s, :], tiles, [zero] * FACES)

    def tile_look(slot, t, seams):
        spread = from_seam(t)
        return look(lambda s: ext[slot, t, 2 + s : 10 + s, :], t, [take(e, spread) for e in seams])

    pairs = chebyshev()
    for step in range(ITERS):
        wait_recv(step)
        seams = seam_look(step)

        if step < ITERS - 1:
            keep, add = pairs[step]

            def advance(t, grown):
                near = tile_look(step, t, seams)
                direction = ext[step, t, 8:16, :]
                z = zed[t] - direction
                for f in range(FACES):
                    z = z + coef[f, t] * near[f]
                    nears[f, t] = near[f] if step == 0 else nears[f, t] + near[f]
                zed[t] = z
                direction = keep * direction + add * z
                total[t] = total[t] + direction
                ext[step + 1, t, 8:16, :] = direction
                return to_seam(t, direction, grown)

            ext[step + 1, tiles, 8:16, :] = lax.fori_loop(0, tiles, advance, zero, unroll=UNROLL)
            start(step + 1)
            wait_send(step)
        else:
            loads[6].wait()

            def finish(t, top):
                near = tile_look(step, t, seams)
                value = total[t]
                p_out[:, cols(t)] = value
                drop = [value - (nears[f, t] + near[f]) for f in range(FACES)]
                rate = zero
                for f in range(FACES):
                    flux = hodge[f, 0, :, cols(t)] * drop[0]
                    for g in range(1, FACES):
                        flux = flux + hodge[f, g, :, cols(t)] * drop[g]
                    fast = jnp.abs(perm[:, cols(t)] * flux)
                    speed[f, t] = fast
                    rate = rate + fast
                return jnp.maximum(top, rate / pv[:, cols(t)])

            peak[0] = lax.fori_loop(0, tiles, finish, zero, unroll=UNROLL)

    def z_copy(k):
        return pltpu.make_async_remote_copy(
            src_ref=peak.at[0], dst_ref=peaks_z.at[k - 1],
            send_sem=pz_send.at[k - 1], recv_sem=pz_recv.at[k - 1],
            device_id=(lax.rem(gz + k, nz), xy), device_id_type=MESH,
        )

    def x_copy(k):
        return pltpu.make_async_remote_copy(
            src_ref=peak.at[1], dst_ref=peaks_x.at[k - 1],
            send_sem=px_send.at[k - 1], recv_sem=px_recv.at[k - 1],
            device_id=(gz, lax.rem(xy + k, nx)), device_id_type=MESH,
        )

    for k in range(1, nz):
        z_copy(k).start()
    loads[7].wait()
    loads[8].wait()
    for k in range(1, nz):
        z_copy(k).wait_recv()
    top = peak[0]
    for k in range(1, nz):
        top = jnp.maximum(top, peaks_z[k - 1])
    peak[1] = top
    for k in range(1, nx):
        x_copy(k).start()

    def inflow(n, t, seams):
        near = tile_look(ITERS + n, t, seams)
        here = -ext[ITERS + n, t, 8:16, :]
        gained = zero
        for f in range(FACES):
            gained = gained + speed[f, t] * jnp.where(up[n, f, :, cols(t)] != 0, near[f], here)
        return gained

    wait_recv(ITERS)
    seams0 = seam_look(ITERS)

    def first_inflow(t, carry):
        grow[t] = inflow(0, t, seams0)
        return carry

    lax.fori_loop(0, tiles, first_inflow, 0, unroll=UNROLL)

    for k in range(1, nx):
        x_copy(k).wait_recv()
    for k in range(1, nx):
        top = jnp.maximum(top, peaks_x[k - 1])
    top = jnp.max(jnp.max(top, axis=1, keepdims=True), axis=0, keepdims=True)
    tau = jnp.broadcast_to(0.8 / top, (8, LANES))

    def first_step(t, grown):
        scale = act[:, cols(t)].astype(jnp.float32) * tau / pv[:, cols(t)]
        gain[t] = scale
        value = sat[:, cols(t)] + scale * grow[t]
        sat[:, cols(t)] = value
        value = fraction(value)
        ext[ITERS + 1, t, 8:16, :] = value
        return to_seam(t, value, grown)

    ext[ITERS + 1, tiles, 8:16, :] = lax.fori_loop(0, tiles, first_step, zero, unroll=UNROLL)
    start(ITERS + 1)
    wait_send(ITERS - 1)
    wait_send(ITERS)
    for k in range(1, nz):
        z_copy(k).wait_send()
    for k in range(1, nx):
        x_copy(k).wait_send()

    for n in range(1, NSUB):
        slot = ITERS + n
        wait_recv(slot)
        seams = seam_look(slot)
        if n < NSUB - 1:
            def substep(t, grown):
                value = sat[:, cols(t)] + gain[t] * inflow(n, t, seams)
                sat[:, cols(t)] = value
                value = fraction(value)
                ext[slot + 1, t, 8:16, :] = value
                return to_seam(t, value, grown)

            ext[slot + 1, tiles, 8:16, :] = lax.fori_loop(0, tiles, substep, zero, unroll=UNROLL)
            start(slot + 1)
        else:
            def last(t, carry):
                s_out[:, cols(t)] = sat[:, cols(t)] + gain[t] * inflow(n, t, seams)
                return carry

            lax.fori_loop(0, tiles, last, 0, unroll=UNROLL)
        wait_send(slot)


def per_device(nz, nx, *args):
    rows, columns = args[1].shape
    tiles = columns // LANES
    slots = ITERS + NSUB
    f32, i32 = jnp.float32, jnp.int32
    scratch = [pltpu.VMEM(a.shape, a.dtype) for a in args]
    plain = (tiles, rows, LANES)
    faces = (FACES, tiles, rows, LANES)
    scratch += [
        pltpu.VMEM((slots, tiles + 1, 3 * rows, LANES), f32),
        pltpu.VMEM((slots, 2, rows, LANES), f32),
        pltpu.VMEM((3 * rows, LANES), f32),
        pltpu.VMEM((FACES, tiles + 1, rows, LANES), i32),
        pltpu.VMEM((FACES, tiles + 1, rows, LANES), i32),
        pltpu.VMEM(faces, f32),
        pltpu.VMEM(plain, f32),
        pltpu.VMEM(plain, f32),
        pltpu.VMEM(faces, f32),
        pltpu.VMEM(faces, f32),
        pltpu.VMEM(plain, f32),
        pltpu.VMEM(plain, f32),
        pltpu.VMEM((2, rows, LANES), f32),
        pltpu.VMEM((nz - 1, rows, LANES), f32),
        pltpu.VMEM((nx - 1, rows, LANES), f32),
        pltpu.SemaphoreType.DMA((len(args),)),
        pltpu.SemaphoreType.DMA((slots, 4)),
        pltpu.SemaphoreType.DMA((slots, 4)),
        pltpu.SemaphoreType.DMA((nz - 1,)),
        pltpu.SemaphoreType.DMA((nz - 1,)),
        pltpu.SemaphoreType.DMA((nx - 1,)),
        pltpu.SemaphoreType.DMA((nx - 1,)),
    ]
    block = jax.ShapeDtypeStruct((rows, columns), f32)
    return tuple(
        pl.pallas_call(
            functools.partial(kernel, nz, nx, tiles),
            out_shape=(block, block),
            in_specs=[pl.BlockSpec(memory_space=pl.ANY)] * len(args),
            out_specs=(pl.BlockSpec(memory_space=pltpu.VMEM),) * 2,
            scratch_shapes=scratch,
            compiler_params=pltpu.CompilerParams(
                collective_id=0, has_side_effects=True, vmem_limit_bytes=32 * 1024 * 1024
            ),
        )(*args)
    )


def solution(mesh):
    placed = (
        P(None, None, "gz", "xy"),
        P("gz", "xy"),
        P("gz", "xy"),
        P("gz", "xy"),
        P("gz", "xy"),
        P("gz", "xy"),
        P(None, "gz", "xy"),
        P(None, None, "gz", "xy"),
        P("gz", "xy"),
    )
    return jax.shard_map(
        functools.partial(per_device, mesh.shape["gz"], mesh.shape["xy"]),
        mesh=mesh,
        in_specs=placed,
        out_specs=(P("gz", "xy"), P("gz", "xy")),
        check_vma=False,
    )
```

```python
import functools

import jax
import jax.numpy as jnp
from jax import lax
from jax.experimental import pallas as pl
from jax.experimental.pallas import tpu as pltpu
from jax.sharding import PartitionSpec as P

REACH = 6
SPAN = 2 * REACH + 1
ITERS = 4
NSUB = 8
FACES = 4
LANES = 128
EDGE = 2 * REACH
NEVER = 99
MESH = pl.DeviceIdType.MESH
SENT = ITERS + NSUB
SAT = ITERS
GAIN = ITERS + 1
FRAC0 = SENT
FRAC1 = SENT + 1


def fraction(sat):
    return sat * sat / (sat * sat + 0.5 * (1.0 - sat) * (1.0 - sat))


def chebyshev():
    sigma = 1.0 / 0.9
    rho = 1.0 / sigma
    pairs = []
    for _ in range(ITERS - 1):
        rho_new = 1.0 / (2.0 * sigma - rho)
        pairs.append((rho_new * rho, 2.0 * rho_new / 0.9))
        rho = rho_new
    return pairs


def take(tile, index):
    return jnp.take_along_axis(tile, index, axis=1, mode="promise_in_bounds")


def kernel(
    nz, nx, tiles,
    hodge_h, perm_h, stor_h, pv_h, src_h, sat_h, near_h, up_h, act_h,
    p_out, s_out,
    hodge, perm, stor, pv, src, sat, code, up, act,
    own, halo, sides, outer, rcode, gindex, coef, zed, total, nears, near0, speed, acc, gain,
    peak, peaks_z, peaks_x,
    load_sem, send_sem, recv_sem, pz_send, pz_recv, px_send, px_recv,
):
    gz = lax.axis_index("gz")
    xy = lax.axis_index("xy")
    loads = [
        pltpu.make_async_copy(a, b, load_sem.at[i])
        for i, (a, b) in enumerate(
            [(sat_h, sat), (near_h, code), (hodge_h, hodge), (perm_h, perm), (stor_h, stor),
             (src_h, src), (pv_h, pv), (act_h, act), (up_h, up)]
        )
    ]
    for load in loads:
        load.start()

    barrier = pltpu.get_barrier_semaphore()
    for k in range(1, nz):
        pl.semaphore_signal(barrier, inc=1, device_id=(lax.rem(gz + k, nz), xy), device_id_type=MESH)
    for k in range(1, nx):
        pl.semaphore_signal(barrier, inc=1, device_id=(gz, lax.rem(xy + k, nx)), device_id_type=MESH)

    lane = lax.broadcasted_iota(jnp.int32, (8, LANES), 1)
    row = lax.broadcasted_iota(jnp.int32, (8, LANES), 0)

    def cols(t):
        return pl.ds(pl.multiple_of(t * LANES, LANES), LANES)

    def to_seam(t, tile, into):
        u = lane - (EDGE * t + REACH)
        index = jnp.where(u < REACH, u, u + (LANES - EDGE)) & (LANES - 1)
        return jnp.where((u >= 0) & (u < EDGE), take(tile, index), into)

    def from_seam(t):
        inner = jnp.where(lane >= LANES - REACH, lane + (EDGE * t + EDGE + REACH - LANES), LANES - 1)
        return jnp.where(lane < REACH, lane + (EDGE * t + REACH), inner)

    def copy(slot, side):
        source, target, device = (
            (own.at[slot, :, 0:8, :], halo.at[slot, :, 8:16, :], (gz - 1, xy)),
            (own.at[slot, :, 0:8, :], halo.at[slot, :, 0:8, :], (gz + 1, xy)),
            (own.at[slot, tiles, 0:8, :], sides.at[slot, 1], (gz, xy - 1)),
            (own.at[slot, tiles, 0:8, :], sides.at[slot, 0], (gz, xy + 1)),
        )[side]
        return pltpu.make_async_remote_copy(
            src_ref=source, dst_ref=target,
            send_sem=send_sem.at[slot, side], recv_sem=recv_sem.at[slot, side],
            device_id=device, device_id_type=MESH,
        )

    has = (gz > 0, gz < nz - 1, xy > 0, xy < nx - 1)

    def start(slot):
        for side in (2, 3, 0, 1):
            @pl.when(has[side])
            def _():
                copy(slot, side).start()

    def wait_send(slot):
        for side in range(4):
            @pl.when(has[side])
            def _():
                copy(slot, side).wait_send()

    def wait_recv(slot, across):
        for side in (2, 3) if across else (0, 1):
            @pl.when(has[side ^ 1])
            def _():
                copy(slot, side).wait_recv()

    zero = jnp.zeros((8, LANES), jnp.float32)

    def over(body, begin, first=0, last=tiles):
        return lax.fori_loop(first, last, body, begin, unroll=last - first)

    def put(slot, t, value):
        own[slot, t, 0:8, :] = value
        own[slot, t, 8:16, :] = value

    loads[0].wait()

    def first_sat(t, seams):
        value = sat[:, cols(t)]
        put(SAT, t, value)
        put(FRAC0, t, fraction(value))
        return to_seam(t, value, seams)

    value = over(first_sat, zero)
    put(SAT, tiles, value)
    put(FRAC0, tiles, fraction(value))
    pl.semaphore_wait(barrier, nz + nx - 2)

    for load in loads[1:6]:
        load.wait()

    def setup(t, seams):
        weights = []
        for g in range(FACES):
            summed = hodge[0, g, :, cols(t)]
            for f in range(1, FACES):
                summed = summed + hodge[f, g, :, cols(t)]
            weights.append(perm[:, cols(t)] * summed)
        diag = stor[:, cols(t)] + (weights[0] + weights[1] + weights[2] + weights[3])
        for g in range(FACES):
            coef[g, t] = weights[g] / diag
        first = src[:, cols(t)] / diag
        zed[t] = first
        total[t] = first
        put(0, t, first)
        return to_seam(t, first, seams)

    put(0, tiles, over(setup, zero))
    start(0)
    start(SAT)

    def rows_code(value):
        return (value * 79) >> 10

    def outside(rc):
        at = row + rc - REACH
        return ((gz == 0) & (at < 0)) | ((gz == nz - 1) & (at >= 8))

    def key(rc):
        at = row + rc - REACH
        turn = (rc - REACH) & 7
        return jnp.where((at >= 0) & (at < 8), turn, turn + 8)

    def codes(t, seams):
        grown = []
        for f in range(FACES):
            value = code[f, :, cols(t)]
            rc = rows_code(value)
            col = lane + (value - SPAN * rc - REACH)
            cross = (col < 0) | (col >= LANES)
            gindex[f, t] = col & (LANES - 1)
            rcode[f, t] = jnp.where(cross | outside(rc), NEVER, key(rc))
            grown.append(to_seam(t, value, seams[f]))
        return tuple(grown)

    seam_codes = lax.fori_loop(0, tiles, codes, (jnp.zeros((8, LANES), jnp.int32),) * FACES)
    for f in range(FACES):
        value = seam_codes[f]
        rc = rows_code(value)
        shift = value - SPAN * rc - REACH
        base = EDGE * ((lane * 43) >> 9)
        here = lane - base
        there = here + shift
        cross = jnp.where(here < REACH, there - REACH, REACH - 1 - there) >= 0
        ours = (lane >= REACH) & (lane < EDGE * tiles + REACH)
        left = (base == 0) & (there < REACH)
        right = (base == EDGE * tiles) & (there >= REACH)
        inside = jnp.logical_not(((xy == 0) & left) | ((xy == nx - 1) & right))
        rows = jnp.where(left | right, key(rc) + 16, key(rc))
        gindex[f, tiles] = (lane + shift) & (LANES - 1)
        rcode[f, tiles] = jnp.where(cross & ours & inside & jnp.logical_not(outside(rc)), rows, NEVER)

    def look(load, t, begin, first, last):
        out = list(begin)
        index = [gindex[f, t] for f in range(FACES)]
        rows = [rcode[f, t] for f in range(FACES)]
        for s in range(first, last):
            x = load(s & 7)
            for f in range(FACES):
                out[f] = jnp.where(rows[f] == s, take(x, index[f]), out[f])
        return out

    def look_here(slot):
        def body(t, carry):
            near = look(lambda q: own[slot, t, pl.ds(q, 8), :], t, [zero] * FACES, 0, 8)
            for f in range(FACES):
                acc[f, t] = near[f]
            return carry

        over(body, 0, 0, tiles + 1)

    def look_rows(slot, t):
        return look(
            lambda q: halo[slot, t, pl.ds(q, 8), :], t, [acc[f, t] for f in range(FACES)], 9, 16
        )

    def spread(seams, t):
        index = from_seam(t)
        return [take(e, index) for e in seams]

    def look_sides(seams, left, right):
        value = jnp.where(
            lane < REACH,
            take(left, (lane + EDGE * tiles) & (LANES - 1)),
            take(right, (lane - EDGE * tiles) & (LANES - 1)),
        )
        outer[0:8, :] = value
        outer[8:16, :] = value
        return look(lambda q: outer[pl.ds(q, 8), :], tiles, seams, 16, 24)

    def near_step(slot, arrive, finish, begin, while_waiting=None):
        look_here(slot)
        if while_waiting is not None:
            while_waiting()
        arrive(False)
        seams = look_rows(slot, tiles)

        def body(t, carry):
            rows = look_rows(slot, t)
            near = [a + b for a, b in zip(rows, spread(seams, t))]
            return finish(t, near, carry)

        carry = over(body, begin, 1, tiles - 1)
        ends = [(t, look_rows(slot, t)) for t in (0, tiles - 1)]
        left, right = arrive(True)
        seams = look_sides(seams, left, right)
        for t, rows in ends:
            near = [a + b for a, b in zip(rows, spread(seams, t))]
            carry = finish(t, near, carry)
        return carry

    def arrived(slot):
        def arrive(across):
            wait_recv(slot, across)
            return (sides[slot, 0], sides[slot, 1]) if across else None

        return arrive

    def arrive_first(across):
        wait_recv(SAT, across)
        if across:
            return fraction(sides[SAT, 0]), fraction(sides[SAT, 1])

        def body(t, carry):
            halo[FRAC0, t] = fraction(halo[SAT, t])
            return carry

        over(body, 0, 0, tiles + 1)

    def first_near():
        def finish(t, near, carry):
            for f in range(FACES):
                near0[f, t] = near[f]
            return carry

        near_step(FRAC0, arrive_first, finish, 0)

    pairs = chebyshev()
    for step in range(ITERS):
        if step < ITERS - 1:
            keep, add = pairs[step]

            def advance(t, near, grown):
                direction = own[step, t, 0:8, :]
                z = zed[t] - direction
                for f in range(FACES):
                    z = z + coef[f, t] * near[f]
                    nears[f, t] = near[f] if step == 0 else nears[f, t] + near[f]
                zed[t] = z
                direction = keep * direction + add * z
                total[t] = total[t] + direction
                put(step + 1, t, direction)
                return to_seam(t, direction, grown)

            put(step + 1, tiles, near_step(step, arrived(step), advance, zero))
            start(step + 1)
            wait_send(step)
            if step == 0:
                first_near()
        else:
            loads[6].wait()

            def flow(t, near, top):
                value = total[t]
                p_out[:, cols(t)] = value
                drop = [value - (nears[f, t] + near[f]) for f in range(FACES)]
                rate = zero
                for f in range(FACES):
                    flux = hodge[f, 0, :, cols(t)] * drop[0]
                    for g in range(1, FACES):
                        flux = flux + hodge[f, g, :, cols(t)] * drop[g]
                    fast = jnp.abs(perm[:, cols(t)] * flux)
                    speed[f, t] = fast
                    rate = rate + fast
                return jnp.maximum(top, rate / pv[:, cols(t)])

            peak[0] = near_step(step, arrived(step), flow, zero)

    def z_copy(k):
        return pltpu.make_async_remote_copy(
            src_ref=peak.at[0], dst_ref=peaks_z.at[k - 1],
            send_sem=pz_send.at[k - 1], recv_sem=pz_recv.at[k - 1],
            device_id=(lax.rem(gz + k, nz), xy), device_id_type=MESH,
        )

    def x_copy(k):
        return pltpu.make_async_remote_copy(
            src_ref=peak.at[1], dst_ref=peaks_x.at[k - 1],
            send_sem=px_send.at[k - 1], recv_sem=px_recv.at[k - 1],
            device_id=(gz, lax.rem(xy + k, nx)), device_id_type=MESH,
        )

    for k in range(1, nz):
        z_copy(k).start()
    loads[7].wait()
    loads[8].wait()

    def inflow(n, slot, t, near):
        here = -own[slot, t, 0:8, :]
        gained = zero
        for f in range(FACES):
            gained = gained + speed[f, t] * jnp.where(up[n, f, :, cols(t)] != 0, near[f], here)
        return gained

    def first_gain(t, grown):
        scale = act[:, cols(t)].astype(jnp.float32) / pv[:, cols(t)]
        gain[t] = scale
        value = scale * inflow(0, FRAC0, t, [near0[f, t] for f in range(FACES)])
        put(GAIN, t, value)
        return to_seam(t, value, grown)

    put(GAIN, tiles, over(first_gain, zero))
    start(GAIN)
    for k in range(1, nz):
        z_copy(k).wait_recv()
    top = peak[0]
    for k in range(1, nz):
        top = jnp.maximum(top, peaks_z[k - 1])
    peak[1] = top
    for k in range(1, nx):
        x_copy(k).start()
    wait_send(ITERS - 1)
    wait_send(SAT)
    for k in range(1, nz):
        z_copy(k).wait_send()
    for k in range(1, nx):
        x_copy(k).wait_recv()
    for k in range(1, nx):
        top = jnp.maximum(top, peaks_x[k - 1])
    top = jnp.max(jnp.max(top, axis=1, keepdims=True), axis=0, keepdims=True)
    tau = jnp.broadcast_to(0.8 / top, (8, LANES))

    def first_step(t, carry):
        gain[t] = gain[t] * tau
        value = sat[:, cols(t)] + tau * own[GAIN, t, 0:8, :]
        sat[:, cols(t)] = value
        put(FRAC1, t, fraction(value))
        return carry

    over(first_step, 0)
    put(FRAC1, tiles, fraction(own[SAT, tiles, 0:8, :] + tau * own[GAIN, tiles, 0:8, :]))

    def arrive_second(across):
        wait_recv(GAIN, across)
        if across:
            return tuple(fraction(sides[SAT, i] + tau * sides[GAIN, i]) for i in range(2))

        def body(t, carry):
            for part in (slice(0, 8), slice(8, 16)):
                halo[FRAC1, t, part, :] = fraction(halo[SAT, t, part, :] + tau * halo[GAIN, t, part, :])
            return carry

        over(body, 0, 0, tiles + 1)

    for n in range(1, NSUB):
        slot = FRAC1 if n == 1 else ITERS + n
        arrive = arrive_second if n == 1 else arrived(slot)
        if n < NSUB - 1:
            def substep(t, near, grown):
                value = sat[:, cols(t)] + gain[t] * inflow(n, slot, t, near)
                sat[:, cols(t)] = value
                value = fraction(value)
                put(ITERS + n + 1, t, value)
                return to_seam(t, value, grown)

            put(ITERS + n + 1, tiles, near_step(slot, arrive, substep, zero))
            start(ITERS + n + 1)
        else:
            def last(t, near, carry):
                s_out[:, cols(t)] = sat[:, cols(t)] + gain[t] * inflow(n, slot, t, near)
                return carry

            near_step(slot, arrive, last, 0)
        wait_send(GAIN if n == 1 else slot)
    for k in range(1, nx):
        x_copy(k).wait_send()


def per_device(nz, nx, *args):
    rows, columns = args[1].shape
    tiles = columns // LANES
    slots = SENT + 2
    f32, i32 = jnp.float32, jnp.int32
    scratch = [pltpu.VMEM(a.shape, a.dtype) for a in args]
    plain = (tiles, rows, LANES)
    faces = (FACES, tiles, rows, LANES)
    scratch += [
        pltpu.VMEM((slots, tiles + 1, 2 * rows, LANES), f32),
        pltpu.VMEM((slots, tiles + 1, 2 * rows, LANES), f32),
        pltpu.VMEM((SENT, 2, rows, LANES), f32),
        pltpu.VMEM((2 * rows, LANES), f32),
        pltpu.VMEM((FACES, tiles + 1, rows, LANES), i32),
        pltpu.VMEM((FACES, tiles + 1, rows, LANES), i32),
        pltpu.VMEM(faces, f32),
        pltpu.VMEM(plain, f32),
        pltpu.VMEM(plain, f32),
        pltpu.VMEM(faces, f32),
        pltpu.VMEM(faces, f32),
        pltpu.VMEM(faces, f32),
        pltpu.VMEM((FACES, tiles + 1, rows, LANES), f32),
        pltpu.VMEM(plain, f32),
        pltpu.VMEM((2, rows, LANES), f32),
        pltpu.VMEM((nz - 1, rows, LANES), f32),
        pltpu.VMEM((nx - 1, rows, LANES), f32),
        pltpu.SemaphoreType.DMA((len(args),)),
        pltpu.SemaphoreType.DMA((SENT, 4)),
        pltpu.SemaphoreType.DMA((SENT, 4)),
        pltpu.SemaphoreType.DMA((nz - 1,)),
        pltpu.SemaphoreType.DMA((nz - 1,)),
        pltpu.SemaphoreType.DMA((nx - 1,)),
        pltpu.SemaphoreType.DMA((nx - 1,)),
    ]
    block = jax.ShapeDtypeStruct((rows, columns), f32)
    return tuple(
        pl.pallas_call(
            functools.partial(kernel, nz, nx, tiles),
            out_shape=(block, block),
            in_specs=[pl.BlockSpec(memory_space=pl.ANY)] * len(args),
            out_specs=(pl.BlockSpec(memory_space=pltpu.VMEM),) * 2,
            scratch_shapes=scratch,
            compiler_params=pltpu.CompilerParams(
                collective_id=0, has_side_effects=True, vmem_limit_bytes=60 * 1024 * 1024
            ),
        )(*args)
    )


def solution(mesh):
    placed = (
        P(None, None, "gz", "xy"),
        P("gz", "xy"),
        P("gz", "xy"),
        P("gz", "xy"),
        P("gz", "xy"),
        P("gz", "xy"),
        P(None, "gz", "xy"),
        P(None, None, "gz", "xy"),
        P("gz", "xy"),
    )
    return jax.shard_map(
        functools.partial(per_device, mesh.shape["gz"], mesh.shape["xy"]),
        mesh=mesh,
        in_specs=placed,
        out_specs=(P("gz", "xy"), P("gz", "xy")),
        check_vma=False,
    )
```

```python
import functools

import jax
import jax.numpy as jnp
from jax import lax
from jax.experimental import pallas as pl
from jax.experimental.pallas import tpu as pltpu
from jax.sharding import PartitionSpec as P

REACH = 6
SPAN = 2 * REACH + 1
ITERS = 4
NSUB = 8
FACES = 4
LANES = 128
EDGE = 2 * REACH
NEVER = 99
MESH = pl.DeviceIdType.MESH
SENT = ITERS + NSUB
SAT = ITERS
GAIN = ITERS + 1
FRAC0 = SENT
FRAC1 = SENT + 1


def fraction(sat):
    return sat * sat / (sat * sat + 0.5 * (1.0 - sat) * (1.0 - sat))


def chebyshev():
    sigma = 1.0 / 0.9
    rho = 1.0 / sigma
    pairs = []
    for _ in range(ITERS - 1):
        rho_new = 1.0 / (2.0 * sigma - rho)
        pairs.append((rho_new * rho, 2.0 * rho_new / 0.9))
        rho = rho_new
    return pairs


def take(tile, index):
    return jnp.take_along_axis(tile, index, axis=1, mode="promise_in_bounds")


def kernel(
    nz, nx, tiles,
    hodge_h, perm_h, stor_h, pv_h, src_h, sat_h, near_h, up_h, act_h,
    p_out, s_out,
    hodge, perm, stor, pv, src, sat, code, up, act,
    own, halo, sides, outer, rcode, gindex, coef, zed, total, nears, near0, speed, acc, gain,
    peak, peaks_z, peaks_x,
    load_sem, send_sem, recv_sem, pz_send, pz_recv, px_send, px_recv,
):
    gz = lax.axis_index("gz")
    xy = lax.axis_index("xy")
    loads = [
        pltpu.make_async_copy(a, b, load_sem.at[i])
        for i, (a, b) in enumerate(
            [(sat_h, sat), (near_h, code), (hodge_h, hodge), (perm_h, perm), (stor_h, stor),
             (src_h, src), (pv_h, pv), (act_h, act), (up_h, up)]
        )
    ]
    for load in loads:
        load.start()

    barrier = pltpu.get_barrier_semaphore()
    for k in range(1, nz):
        pl.semaphore_signal(barrier, inc=1, device_id=(lax.rem(gz + k, nz), xy), device_id_type=MESH)
    for k in range(1, nx):
        pl.semaphore_signal(barrier, inc=1, device_id=(gz, lax.rem(xy + k, nx)), device_id_type=MESH)

    lane = lax.broadcasted_iota(jnp.int32, (8, LANES), 1)
    row = lax.broadcasted_iota(jnp.int32, (8, LANES), 0)

    def cols(t):
        return pl.ds(pl.multiple_of(t * LANES, LANES), LANES)

    def to_seam(t, tile, into):
        u = lane - (EDGE * t + REACH)
        index = jnp.where(u < REACH, u, u + (LANES - EDGE)) & (LANES - 1)
        return jnp.where((u >= 0) & (u < EDGE), take(tile, index), into)

    def from_seam(t):
        inner = jnp.where(lane >= LANES - REACH, lane + (EDGE * t + EDGE + REACH - LANES), LANES - 1)
        return jnp.where(lane < REACH, lane + (EDGE * t + REACH), inner)

    def copy(slot, side):
        source, target, device = (
            (own.at[slot, :, 0:8, :], halo.at[slot, :, 8:16, :], (gz - 1, xy)),
            (own.at[slot, :, 0:8, :], halo.at[slot, :, 0:8, :], (gz + 1, xy)),
            (own.at[slot, tiles, 0:8, :], sides.at[slot, 1], (gz, xy - 1)),
            (own.at[slot, tiles, 0:8, :], sides.at[slot, 0], (gz, xy + 1)),
        )[side]
        return pltpu.make_async_remote_copy(
            src_ref=source, dst_ref=target,
            send_sem=send_sem.at[slot, side], recv_sem=recv_sem.at[slot, side],
            device_id=device, device_id_type=MESH,
        )

    has = (gz > 0, gz < nz - 1, xy > 0, xy < nx - 1)

    def start(slot):
        for side in (2, 3, 0, 1):
            @pl.when(has[side])
            def _():
                copy(slot, side).start()

    def wait_send(slot):
        for side in range(4):
            @pl.when(has[side])
            def _():
                copy(slot, side).wait_send()

    def wait_recv(slot, across):
        for side in (2, 3) if across else (0, 1):
            @pl.when(has[side ^ 1])
            def _():
                copy(slot, side).wait_recv()

    zero = jnp.zeros((8, LANES), jnp.float32)

    def over(body, begin, first=0, last=tiles):
        return lax.fori_loop(first, last, body, begin, unroll=last - first)

    def put(slot, t, value):
        own[slot, t, 0:8, :] = value
        own[slot, t, 8:16, :] = value

    loads[0].wait()

    def first_sat(t, seams):
        value = sat[:, cols(t)]
        put(SAT, t, value)
        put(FRAC0, t, fraction(value))
        return to_seam(t, value, seams)

    value = over(first_sat, zero)
    put(SAT, tiles, value)
    put(FRAC0, tiles, fraction(value))
    pl.semaphore_wait(barrier, nz + nx - 2)

    for load in loads[1:6]:
        load.wait()

    def setup(t, seams):
        weights = []
        for g in range(FACES):
            summed = hodge[0, g, :, cols(t)]
            for f in range(1, FACES):
                summed = summed + hodge[f, g, :, cols(t)]
            weights.append(perm[:, cols(t)] * summed)
        diag = stor[:, cols(t)] + (weights[0] + weights[1] + weights[2] + weights[3])
        for g in range(FACES):
            coef[g, t] = weights[g] / diag
        first = src[:, cols(t)] / diag
        zed[t] = first
        total[t] = first
        put(0, t, first)
        return to_seam(t, first, seams)

    put(0, tiles, over(setup, zero))
    start(0)
    start(SAT)

    def rows_code(value):
        return (value * 79) >> 10

    def outside(rc):
        at = row + rc - REACH
        return ((gz == 0) & (at < 0)) | ((gz == nz - 1) & (at >= 8))

    def key(rc):
        at = row + rc - REACH
        turn = (rc - REACH) & 7
        return jnp.where((at >= 0) & (at < 8), turn, turn + 8)

    def codes(t, seams):
        grown = []
        for f in range(FACES):
            value = code[f, :, cols(t)]
            rc = rows_code(value)
            col = lane + (value - SPAN * rc - REACH)
            cross = (col < 0) | (col >= LANES)
            gindex[f, t] = col & (LANES - 1)
            rcode[f, t] = jnp.where(cross | outside(rc), NEVER, key(rc))
            grown.append(to_seam(t, value, seams[f]))
        return tuple(grown)

    seam_codes = lax.fori_loop(0, tiles, codes, (jnp.zeros((8, LANES), jnp.int32),) * FACES)
    for f in range(FACES):
        value = seam_codes[f]
        rc = rows_code(value)
        shift = value - SPAN * rc - REACH
        base = EDGE * ((lane * 43) >> 9)
        here = lane - base
        there = here + shift
        cross = jnp.where(here < REACH, there - REACH, REACH - 1 - there) >= 0
        ours = (lane >= REACH) & (lane < EDGE * tiles + REACH)
        left = (base == 0) & (there < REACH)
        right = (base == EDGE * tiles) & (there >= REACH)
        inside = jnp.logical_not(((xy == 0) & left) | ((xy == nx - 1) & right))
        rows = jnp.where(left | right, key(rc) + 16, key(rc))
        gindex[f, tiles] = (lane + shift) & (LANES - 1)
        rcode[f, tiles] = jnp.where(cross & ours & inside & jnp.logical_not(outside(rc)), rows, NEVER)

    def look(load, t, begin, first, last):
        out = list(begin)
        index = [gindex[f, t] for f in range(FACES)]
        rows = [rcode[f, t] for f in range(FACES)]
        for f in range(FACES):
            for s in range(first, last):
                out[f] = jnp.where(rows[f] == s, take(load(s & 7), index[f]), out[f])
        return out

    def look_here(slot):
        def body(t, carry):
            near = look(lambda q: own[slot, t, pl.ds(q, 8), :], t, [zero] * FACES, 0, 8)
            for f in range(FACES):
                acc[f, t] = near[f]
            return carry

        over(body, 0, 0, tiles + 1)

    def look_rows(slot, t):
        return look(
            lambda q: halo[slot, t, pl.ds(q, 8), :], t, [acc[f, t] for f in range(FACES)], 9, 16
        )

    def spread(seams, t):
        index = from_seam(t)
        return [take(e, index) for e in seams]

    def look_sides(seams, left, right):
        value = jnp.where(
            lane < REACH,
            take(left, (lane + EDGE * tiles) & (LANES - 1)),
            take(right, (lane - EDGE * tiles) & (LANES - 1)),
        )
        outer[0:8, :] = value
        outer[8:16, :] = value
        return look(lambda q: outer[pl.ds(q, 8), :], tiles, seams, 16, 24)

    def near_step(slot, arrive, finish, begin, while_waiting=None):
        look_here(slot)
        if while_waiting is not None:
            while_waiting()
        arrive(False)
        seams = look_rows(slot, tiles)

        def body(t, carry):
            rows = look_rows(slot, t)
            near = [a + b for a, b in zip(rows, spread(seams, t))]
            return finish(t, near, carry)

        carry = over(body, begin, 1, tiles - 1)
        ends = [(t, look_rows(slot, t)) for t in (0, tiles - 1)]
        left, right = arrive(True)
        seams = look_sides(seams, left, right)
        for t, rows in ends:
            near = [a + b for a, b in zip(rows, spread(seams, t))]
            carry = finish(t, near, carry)
        return carry

    def arrived(slot):
        def arrive(across):
            wait_recv(slot, across)
            return (sides[slot, 0], sides[slot, 1]) if across else None

        return arrive

    def arrive_first(across):
        wait_recv(SAT, across)
        if across:
            return fraction(sides[SAT, 0]), fraction(sides[SAT, 1])

        def body(t, carry):
            halo[FRAC0, t] = fraction(halo[SAT, t])
            return carry

        over(body, 0, 0, tiles + 1)

    def first_near():
        def finish(t, near, carry):
            for f in range(FACES):
                near0[f, t] = near[f]
            return carry

        near_step(FRAC0, arrive_first, finish, 0)

    pairs = chebyshev()
    for step in range(ITERS):
        if step < ITERS - 1:
            keep, add = pairs[step]

            def advance(t, near, grown):
                direction = own[step, t, 0:8, :]
                z = zed[t] - direction
                for f in range(FACES):
                    z = z + coef[f, t] * near[f]
                    nears[f, t] = near[f] if step == 0 else nears[f, t] + near[f]
                zed[t] = z
                direction = keep * direction + add * z
                total[t] = total[t] + direction
                put(step + 1, t, direction)
                return to_seam(t, direction, grown)

            put(step + 1, tiles, near_step(step, arrived(step), advance, zero))
            start(step + 1)
            wait_send(step)
            if step == 0:
                first_near()
        else:
            loads[6].wait()

            def flow(t, near, top):
                value = total[t]
                p_out[:, cols(t)] = value
                drop = [value - (nears[f, t] + near[f]) for f in range(FACES)]
                rate = zero
                for f in range(FACES):
                    flux = hodge[f, 0, :, cols(t)] * drop[0]
                    for g in range(1, FACES):
                        flux = flux + hodge[f, g, :, cols(t)] * drop[g]
                    fast = jnp.abs(perm[:, cols(t)] * flux)
                    speed[f, t] = fast
                    rate = rate + fast
                return jnp.maximum(top, rate / pv[:, cols(t)])

            peak[0] = near_step(step, arrived(step), flow, zero)

    def z_copy(k):
        return pltpu.make_async_remote_copy(
            src_ref=peak.at[0], dst_ref=peaks_z.at[k - 1],
            send_sem=pz_send.at[k - 1], recv_sem=pz_recv.at[k - 1],
            device_id=(lax.rem(gz + k, nz), xy), device_id_type=MESH,
        )

    def x_copy(k):
        return pltpu.make_async_remote_copy(
            src_ref=peak.at[1], dst_ref=peaks_x.at[k - 1],
            send_sem=px_send.at[k - 1], recv_sem=px_recv.at[k - 1],
            device_id=(gz, lax.rem(xy + k, nx)), device_id_type=MESH,
        )

    for k in range(1, nz):
        z_copy(k).start()
    loads[7].wait()
    loads[8].wait()

    def inflow(n, slot, t, near):
        here = -own[slot, t, 0:8, :]
        gained = zero
        for f in range(FACES):
            gained = gained + speed[f, t] * jnp.where(up[n, f, :, cols(t)] != 0, near[f], here)
        return gained

    def first_gain(t, grown):
        scale = act[:, cols(t)].astype(jnp.float32) / pv[:, cols(t)]
        gain[t] = scale
        value = scale * inflow(0, FRAC0, t, [near0[f, t] for f in range(FACES)])
        put(GAIN, t, value)
        return to_seam(t, value, grown)

    put(GAIN, tiles, over(first_gain, zero))
    start(GAIN)
    for k in range(1, nz):
        z_copy(k).wait_recv()
    top = peak[0]
    for k in range(1, nz):
        top = jnp.maximum(top, peaks_z[k - 1])
    peak[1] = top
    for k in range(1, nx):
        x_copy(k).start()
    wait_send(ITERS - 1)
    wait_send(SAT)
    for k in range(1, nz):
        z_copy(k).wait_send()
    for k in range(1, nx):
        x_copy(k).wait_recv()
    for k in range(1, nx):
        top = jnp.maximum(top, peaks_x[k - 1])
    top = jnp.max(jnp.max(top, axis=1, keepdims=True), axis=0, keepdims=True)
    tau = jnp.broadcast_to(0.8 / top, (8, LANES))

    def first_step(t, carry):
        gain[t] = gain[t] * tau
        value = sat[:, cols(t)] + tau * own[GAIN, t, 0:8, :]
        sat[:, cols(t)] = value
        put(FRAC1, t, fraction(value))
        return carry

    over(first_step, 0)
    put(FRAC1, tiles, fraction(own[SAT, tiles, 0:8, :] + tau * own[GAIN, tiles, 0:8, :]))

    def arrive_second(across):
        wait_recv(GAIN, across)
        if across:
            return tuple(fraction(sides[SAT, i] + tau * sides[GAIN, i]) for i in range(2))

        def body(t, carry):
            for part in (slice(0, 8), slice(8, 16)):
                halo[FRAC1, t, part, :] = fraction(halo[SAT, t, part, :] + tau * halo[GAIN, t, part, :])
            return carry

        over(body, 0, 0, tiles + 1)

    for n in range(1, NSUB):
        slot = FRAC1 if n == 1 else ITERS + n
        arrive = arrive_second if n == 1 else arrived(slot)
        if n < NSUB - 1:
            def substep(t, near, grown):
                value = sat[:, cols(t)] + gain[t] * inflow(n, slot, t, near)
                sat[:, cols(t)] = value
                value = fraction(value)
                put(ITERS + n + 1, t, value)
                return to_seam(t, value, grown)

            put(ITERS + n + 1, tiles, near_step(slot, arrive, substep, zero))
            start(ITERS + n + 1)
        else:
            def last(t, near, carry):
                s_out[:, cols(t)] = sat[:, cols(t)] + gain[t] * inflow(n, slot, t, near)
                return carry

            near_step(slot, arrive, last, 0)
        wait_send(GAIN if n == 1 else slot)
    for k in range(1, nx):
        x_copy(k).wait_send()


def per_device(nz, nx, *args):
    rows, columns = args[1].shape
    tiles = columns // LANES
    slots = SENT + 2
    f32, i32 = jnp.float32, jnp.int32
    scratch = [pltpu.VMEM(a.shape, a.dtype) for a in args]
    plain = (tiles, rows, LANES)
    faces = (FACES, tiles, rows, LANES)
    scratch += [
        pltpu.VMEM((slots, tiles + 1, 2 * rows, LANES), f32),
        pltpu.VMEM((slots, tiles + 1, 2 * rows, LANES), f32),
        pltpu.VMEM((SENT, 2, rows, LANES), f32),
        pltpu.VMEM((2 * rows, LANES), f32),
        pltpu.VMEM((FACES, tiles + 1, rows, LANES), i32),
        pltpu.VMEM((FACES, tiles + 1, rows, LANES), i32),
        pltpu.VMEM(faces, f32),
        pltpu.VMEM(plain, f32),
        pltpu.VMEM(plain, f32),
        pltpu.VMEM(faces, f32),
        pltpu.VMEM(faces, f32),
        pltpu.VMEM(faces, f32),
        pltpu.VMEM((FACES, tiles + 1, rows, LANES), f32),
        pltpu.VMEM(plain, f32),
        pltpu.VMEM((2, rows, LANES), f32),
        pltpu.VMEM((nz - 1, rows, LANES), f32),
        pltpu.VMEM((nx - 1, rows, LANES), f32),
        pltpu.SemaphoreType.DMA((len(args),)),
        pltpu.SemaphoreType.DMA((SENT, 4)),
        pltpu.SemaphoreType.DMA((SENT, 4)),
        pltpu.SemaphoreType.DMA((nz - 1,)),
        pltpu.SemaphoreType.DMA((nz - 1,)),
        pltpu.SemaphoreType.DMA((nx - 1,)),
        pltpu.SemaphoreType.DMA((nx - 1,)),
    ]
    block = jax.ShapeDtypeStruct((rows, columns), f32)
    return tuple(
        pl.pallas_call(
            functools.partial(kernel, nz, nx, tiles),
            out_shape=(block, block),
            in_specs=[pl.BlockSpec(memory_space=pl.ANY)] * len(args),
            out_specs=(pl.BlockSpec(memory_space=pltpu.VMEM),) * 2,
            scratch_shapes=scratch,
            compiler_params=pltpu.CompilerParams(
                collective_id=0, has_side_effects=True, vmem_limit_bytes=60 * 1024 * 1024
            ),
        )(*args)
    )


def solution(mesh):
    placed = (
        P(None, None, "gz", "xy"),
        P("gz", "xy"),
        P("gz", "xy"),
        P("gz", "xy"),
        P("gz", "xy"),
        P("gz", "xy"),
        P(None, "gz", "xy"),
        P(None, None, "gz", "xy"),
        P("gz", "xy"),
    )
    return jax.shard_map(
        functools.partial(per_device, mesh.shape["gz"], mesh.shape["xy"]),
        mesh=mesh,
        in_specs=placed,
        out_specs=(P("gz", "xy"), P("gz", "xy")),
        check_vma=False,
    )
```
